32 devices in a mesh: gx: 8 (over z, core), gy: 4 (over y, x).
Axes of the slice: x: 2, y: 2, z: 4, core: 2. Of those that a mesh axis runs over, the one named last changes fastest.
Arguments:
- density: float32 [2, 128, 128, 128], P(None, 'gx', 'gy'), may hold values from 0.2 to 1
- cotangent: float32 [2, 128, 128, 128], P(None, 'gx', 'gy'), may hold values from -6 to 6
- adhesion: float32 [2, 2], replicated, may hold values from 1 to 3
Outputs:
- density_bar: float32 [2, 128, 128, 128], P(None, 'gx', 'gy')
The draws below stay inside these ranges and needn't reach their ends.
All inputs are finite; a program needn't handle non-finite values.
Results may differ from the reference program's by a relative error of at most 0.000084.
Values sent between devices are 32-bit elements; how exact they have to be, the bound alone decides.
A program may use at most 64 MiB of HBM per device.

```python
import jax
import jax.numpy as jnp
from jax import lax

RADIUS = 16
CZ = 128
NX = 128
NY = 128


def draw_density(key, part):
    key_rows, key_cols, key_cells = jax.random.split(jax.random.fold_in(key, 11), 3)
    profile_rows = jax.random.uniform(key_rows, (2, NX, 1, 1), jnp.float32, -1.0, 1.0)
    profile_cols = jax.random.uniform(key_cols, (2, 1, NY, 1), jnp.float32, -1.0, 1.0)
    cells = jax.random.uniform(key_cells, (2, NX, NY, CZ), jnp.float32, -1.0, 1.0)
    result = 0.6 + 0.15 * profile_rows + 0.15 * profile_cols + 0.1 * cells
    return result.astype(jnp.float32)


def draw_cotangent(key, part):
    key_rows, key_cols, key_cells = jax.random.split(jax.random.fold_in(key, 23), 3)
    profile_rows = jax.random.uniform(key_rows, (2, NX, 1, 1), jnp.float32, -1.7, 1.7)
    profile_cols = jax.random.uniform(key_cols, (2, 1, NY, 1), jnp.float32, -1.7, 1.7)
    cells = jnp.clip(jax.random.normal(key_cells, (2, NX, NY, CZ), jnp.float32), -4.5, 4.5)
    result = 0.25 * profile_rows + 0.25 * profile_cols + 0.8 * cells
    return result.astype(jnp.float32)


def setup_inputs(seed: int = 0) -> dict:
    seeds = jax.random.split(jax.random.key(seed), 4)
    density = draw_density(jax.random.fold_in(seeds[3], 71), 0)
    cotangent = draw_cotangent(jax.random.fold_in(seeds[3], 71), 0)
    adhesion = jnp.clip(jax.random.uniform(seeds[2], (2, 2), jnp.float32, 1.0, 3.0), 1.0, 3.0)
    return dict(density=density, cotangent=cotangent, adhesion=adhesion)


time_step = 0.5
smoothing = 0.1

def kernel_taps(antisym):
    offsets = jnp.arange(-RADIUS, RADIUS + 1).astype(jnp.float32)
    weights = 1.0 - jnp.abs(offsets) / (RADIUS + 1.0)
    if antisym:
        weights = weights * offsets / RADIUS
    return weights / jnp.sqrt(jnp.sum(weights * weights))

def correlate(values, taps, along):
    length = values.shape[along]
    widths = [(0, 0)] * values.ndim
    widths[along] = (RADIUS, RADIUS)
    padded = jnp.pad(values, widths)
    result = jnp.zeros_like(values)
    for offset in range(2 * RADIUS + 1):
        result = result + taps[offset] * lax.slice_in_dim(padded, offset, offset + length, axis=along)
    return result

def face_flux(density, velocity, along):
    length = density.shape[along]
    lower_density = lax.slice_in_dim(density, 0, length - 1, axis=along)
    upper_density = lax.slice_in_dim(density, 1, length, axis=along)
    face_velocity = 0.5 * (lax.slice_in_dim(velocity, 0, length - 1, axis=along) + lax.slice_in_dim(velocity, 1, length, axis=along))
    magnitude = jnp.sqrt(face_velocity * face_velocity + smoothing * smoothing)
    flux_value = face_velocity * 0.5 * (lower_density + upper_density) - magnitude * 0.5 * (upper_density - lower_density)
    widths = [(0, 0)] * density.ndim
    widths[along] = (1, 1)
    padded = jnp.pad(flux_value, widths)
    return lax.slice_in_dim(padded, 1, length + 1, axis=along) - lax.slice_in_dim(padded, 0, length, axis=along)

def adhesion_step(density, potential):
    even_taps = kernel_taps(False)
    odd_taps = kernel_taps(True)
    even_in_z = correlate(potential, even_taps, 2)
    odd_in_z = correlate(potential, odd_taps, 2)
    velocity_x = correlate(correlate(even_in_z, even_taps, 1), odd_taps, 0)
    velocity_y = correlate(correlate(even_in_z, odd_taps, 1), even_taps, 0)
    velocity_z = correlate(correlate(odd_in_z, even_taps, 1), even_taps, 0)
    change = face_flux(density, velocity_x, 0) + face_flux(density, velocity_y, 1) + face_flux(density, velocity_z, 2)
    return density - time_step * change

def reference(density, cotangent, adhesion):
    potential = jnp.stack([adhesion[0, 0] * density[0] + adhesion[0, 1] * density[1], adhesion[1, 0] * density[0] + adhesion[1, 1] * density[1]])

    def per_population(inputs):
        own_density, own_potential, own_cotangent = inputs
        updated, pullback = jax.vjp(adhesion_step, own_density, own_potential)
        return pullback(own_cotangent)
    direct, potential_bar = lax.map(per_population, (density, potential, cotangent))
    return jnp.stack([direct[0] + adhesion[0, 0] * potential_bar[0] + adhesion[1, 0] * potential_bar[1], direct[1] + adhesion[0, 1] * potential_bar[0] + adhesion[1, 1] * potential_bar[1]])
```

```python
import math

import jax
import jax.numpy as jnp
from jax import lax
from jax.experimental import pallas as pl
from jax.experimental.pallas import tpu as pltpu
from jax.sharding import PartitionSpec as P

R = 16
TIME_STEP = 0.5
SMOOTHING = 0.1
MESH = pl.DeviceIdType.MESH
F32 = jnp.float32
BF16 = jnp.bfloat16


def even_int(d):
    return jnp.maximum(R + 1.0 - jnp.abs(d), 0.0)


def odd_int(d):
    return even_int(d) * d


def weight_scale():
    e = sum((R + 1 - abs(d)) ** 2 for d in range(-R, R + 1))
    o = sum(((R + 1 - abs(d)) * d) ** 2 for d in range(-R, R + 1))
    return 1.0 / (math.sqrt(o) * e)


def offsets(rows, cols, lead):
    r = lax.broadcasted_iota(jnp.int32, (rows, cols), 0)
    c = lax.broadcasted_iota(jnp.int32, (rows, cols), 1)
    return (c - r - lead).astype(F32)


def split(v):
    hi = v.astype(BF16)
    return hi, (v - hi.astype(F32)).astype(BF16)


def dot(a, b):
    return lax.dot_general(a, b, (((1,), (0,)), ((), ())), preferred_element_type=F32)


def filter_rows(p, count):
    def box(k):
        s = p[k]
        for j in range(k + 1, k + R + 1):
            s = s + p[j]
        return s

    def start_odd(c):
        s = None
        for d in range(1, R + 1):
            t = float((R + 1 - d) * d) * (p[c + R + d] - p[c + R - d])
            s = t if s is None else s + t
        return s

    e0 = float(R + 1) * p[R]
    for d in range(1, R + 1):
        e0 = e0 + float(R + 1 - d) * (p[R + d] + p[R - d])
    even, odd = [e0], [start_odd(0), start_odd(1)]
    slope = odd[1] - odd[0]
    lo, hi = box(0), box(R + 1)
    for c in range(count - 1):
        if c > 0:
            lo = lo + (p[c + R] - p[c - 1])
            hi = hi + (p[c + 2 * R + 1] - p[c + R])
        delta = hi - lo
        even.append(even[-1] + delta)
        if c > 0:
            slope = slope + (
                (R + 2.0) * p[c + 2 * R + 1] - 2.0 * (delta + p[c + R]) - float(R) * p[c - 1]
            )
            odd.append(odd[-1] + slope)
    return even, odd


def spread_rows(q, p):
    n = len(q)

    def prefix(v):
        c = [None, v[0]]
        for k in range(1, n):
            c.append(c[-1] + v[k])
        return c

    cq, cp = prefix(q), prefix(p)

    def at(c, k):
        return c[min(max(k, 0), n)]

    def total(terms):
        s = None
        for w, v in terms:
            if v is None or w == 0.0:
                continue
            t = v if w == 1.0 else w * v
            s = t if s is None else s + t
        return s

    def plus(a, b):
        if a is None:
            return b
        return a if b is None else a + b

    out, slope, value = [], None, None
    for j in range(-1, n + 2 * R - 1):
        inner = [(1.0, at(cp, j + 1)), (-1.0, at(cp, j - R + 1)), (-1.0, at(cp, j - R)), (1.0, at(cp, j - 2 * R))]
        terms = {}
        for w, v in inner:
            if v is not None:
                terms[id(v)] = (terms.get(id(v), (0.0, v))[0] + 2.0 * w, v)
        terms = list(terms.values())
        if 0 <= j - 2 * R - 1 < n:
            terms.append((float(R), p[j - 2 * R - 1]))
        if 0 <= j + 1 < n:
            terms.append((-float(R), p[j + 1]))
        slope = plus(slope, total(terms))
        terms = {}
        for w, v in [(1.0, at(cq, j + 2)), (-2.0, at(cq, j - R + 1)), (1.0, at(cq, j - 2 * R))]:
            if v is not None:
                terms[id(v)] = (terms.get(id(v), (0.0, v))[0] + w, v)
        value = plus(value, plus(slope, total(list(terms.values()))))
        out.append(value)
    return out


def face_terms(lower_d, upper_d, lower_c, upper_c, lower_v, upper_v, valid):
    f = 0.5 * (lower_v + upper_v)
    square = f * f + SMOOTHING * SMOOTHING
    inverse = lax.rsqrt(square)
    magnitude = square * inverse
    bar = jnp.where(valid, (0.5 * TIME_STEP) * (upper_c - lower_c), 0.0)
    return (
        bar * (f + magnitude),
        bar * (f - magnitude),
        bar * ((lower_d + upper_d) - (f * inverse) * (upper_d - lower_d)),
    )


class Pair:
    def __init__(self, axis, place, src_up, dst_up, src_down, dst_down, send, recv, index, only=None):
        self.lo, self.hi = place["has_lo"], place["has_hi"]
        if only is not None:
            self.lo, self.hi = self.lo & only, self.hi & only
        self.up = pltpu.make_async_remote_copy(
            src_ref=src_up, dst_ref=dst_up, send_sem=send.at[index], recv_sem=recv.at[index],
            device_id={axis: place["hi"]}, device_id_type=MESH)
        self.down = pltpu.make_async_remote_copy(
            src_ref=src_down, dst_ref=dst_down, send_sem=send.at[index + 1], recv_sem=recv.at[index + 1],
            device_id={axis: place["lo"]}, device_id_type=MESH)

    def start(self):
        pl.when(self.hi)(lambda: self.up.start())
        pl.when(self.lo)(lambda: self.down.start())

    def wait_recv(self):
        pl.when(self.lo)(lambda: self.up.wait_recv())
        pl.when(self.hi)(lambda: self.down.wait_recv())

    def wait_send(self):
        pl.when(self.hi)(lambda: self.up.wait_send())
        pl.when(self.lo)(lambda: self.down.wait_send())


def place_on(axis, count):
    me = lax.axis_index(axis)
    return {
        "has_lo": me > 0,
        "has_hi": me < count - 1,
        "lo": jnp.maximum(me - 1, 0),
        "hi": jnp.minimum(me + 1, count - 1),
    }


def kernel(nx, ny, adh, den, cot, out, pot, uv, tri, vx, vyz, zt, dcx, rim_y, stage_y, rim_vy, stage_vy,
           spread, rx, ry, wy, wyt, wz, send, recv):
    X, Y, Z = den.shape[1:]
    XE, YE = X + 2 * R, Y + 2 * R
    gx, gy = place_on("gx", nx), place_on("gy", ny)
    scale = weight_scale()

    barrier = pltpu.get_barrier_semaphore()
    for axis, place in (("gx", gx), ("gy", gy)):
        for has, other in ((place["has_lo"], place["lo"]), (place["has_hi"], place["hi"])):
            @pl.when(has)
            def _():
                pl.semaphore_signal(barrier, inc=1, device_id={axis: other}, device_id_type=MESH)

    def zero(ref):
        ref[...] = jnp.zeros(ref.shape, ref.dtype)

    @pl.when(jnp.logical_not(gx["has_lo"]))
    def _():
        zero(pot.at[:, 0:R])
        zero(rx.at[:, 0])
        zero(dcx.at[:, 0:1])
        zero(vx.at[:, 0:1])

    @pl.when(jnp.logical_not(gx["has_hi"]))
    def _():
        zero(pot.at[:, R + X:])
        zero(rx.at[:, 1])
        zero(dcx.at[:, X + 1:])
        zero(vx.at[:, X + 1:])

    @pl.when(jnp.logical_not(gy["has_lo"]))
    def _():
        zero(pot.at[:, :, 0:R])
        zero(ry.at[:, 0])
        zero(rim_y.at[0])
        zero(rim_vy.at[:, 0])

    @pl.when(jnp.logical_not(gy["has_hi"]))
    def _():
        zero(pot.at[:, :, R + Y:])
        zero(ry.at[:, 1])
        zero(rim_y.at[1])
        zero(rim_vy.at[:, 1])

    a = [[adh[i, j] * scale for j in range(2)] for i in range(2)]

    def mix(x, carry):
        d = [den[0, x], den[1, x]]
        for i in range(2):
            pot[i, R + x, R:R + Y, :] = a[i][0] * d[0] + a[i][1] * d[1]
            dcx[i, 1 + x] = d[i]
            dcx[2 + i, 1 + x] = cot[i, x]
        return carry

    lax.fori_loop(0, X, mix, 0)
    for i in range(2):
        for x in range(X):
            stage_y[0, i, x:x + 1, :] = den[i, x, 0:1, :]
            stage_y[1, i, x:x + 1, :] = den[i, x, Y - 1:Y, :]
            stage_y[0, 2 + i, x:x + 1, :] = cot[i, x, 0:1, :]
            stage_y[1, 2 + i, x:x + 1, :] = cot[i, x, Y - 1:Y, :]

    peers = sum(place[has].astype(jnp.int32) for place in (gx, gy) for has in ("has_lo", "has_hi"))
    pl.semaphore_wait(barrier, peers)

    cx, cy = slice(R, R + X), slice(R, R + Y)
    sends = []
    counter = [0]

    def pair(axis, *refs, only=None):
        index = counter[0]
        counter[0] += 2
        made = Pair(axis, gx if axis == "gx" else gy, *refs, send, recv, index, only)
        sends.append(made)
        return made

    to_y, to_x = [], []
    for i in range(2):
        to_y.append(pair("gy", pot.at[i, cx, Y:Y + R], pot.at[i, cx, 0:R],
                         pot.at[i, cx, R:2 * R], pot.at[i, cx, R + Y:YE]))
        to_x.append(pair("gx", pot.at[i, X:X + R, cy], pot.at[i, 0:R, cy],
                         pot.at[i, R:2 * R, cy], pot.at[i, R + X:XE, cy]))
        to_y[i].start()
        to_x[i].start()
    rims = [
        pair("gx", dcx.at[:, X], dcx.at[:, 0], dcx.at[:, 1], dcx.at[:, X + 1]),
        pair("gy", stage_y.at[1], rim_y.at[0], stage_y.at[0], rim_y.at[1]),
    ]

    o = offsets(Y, YE, R)
    for k in range(2):
        wy[0:Y, k * YE:(k + 1) * YE] = even_int(o).astype(BF16)
        wy[Y:2 * Y, k * YE:(k + 1) * YE] = odd_int(o).astype(BF16)
    o = -offsets(YE, Y, -R)
    for k in range(2):
        wyt[:, k * Y:(k + 1) * Y] = even_int(o).astype(BF16)
        wyt[:, (2 + k) * Y:(3 + k) * Y] = odd_int(o).astype(BF16)
    o = offsets(Z, Z, 0)
    for k in range(2):
        wz[0, k * Z:(k + 1) * Z, :] = even_int(o).astype(BF16)
        wz[1, k * Z:(k + 1) * Z, :] = odd_int(-o).astype(BF16)
        wz[2, k * Z:(k + 1) * Z, :] = odd_int(o).astype(BF16)

    corners = []
    for i in range(2):
        to_y[i].wait_recv()
        made = []
        for part, only in ((slice(0, R), gy["has_lo"]), (slice(R + Y, YE), gy["has_hi"])):
            made.append(pair("gx", pot.at[i, X:X + R, part], pot.at[i, 0:R, part],
                             pot.at[i, R:2 * R, part], pot.at[i, R + X:XE, part], only=only))
            made[-1].start()
        corners.append(made)
        if i == 0:
            for r in rims:
                r.start()

    row = lax.broadcasted_iota(jnp.int32, (Y, Z), 0)
    lane = lax.broadcasted_iota(jnp.int32, (Y, Z), 1)
    valid_z = lane < Z - 1
    valid_y = (row < Y - 1) | gy["has_hi"]

    def forward(i):
        def along_x(k, carry):
            y0 = pl.multiple_of(k * 8, 8)
            p = [pot[i, j, pl.ds(y0, 8), :] for j in range(XE)]
            even, odd = filter_rows(p, X)
            for c in range(X):
                uv[c, pl.ds(y0, 8), 0:Z] = even[c]
                uv[c, pl.ds(y0, 8), Z:2 * Z] = odd[c]
            return carry

        lax.fori_loop(0, YE // 8, along_x, 0)

        def along_y(x, carry):
            hi, lo = split(uv[x])
            r = dot(wy[...], jnp.concatenate([hi, lo], 0))
            rows = pl.ds(pl.multiple_of(x * Y, Y), Y)
            for k, v in enumerate((r[0:Y, Z:], r[Y:, 0:Z], r[0:Y, 0:Z])):
                hi, lo = split(v)
                tri[k, rows, 0:Z] = hi
                tri[k, rows, Z:2 * Z] = lo
            return carry

        lax.fori_loop(0, X, along_y, 0, unroll=2)
        vx[i, 1:X + 1] = dot(tri[0], wz[0]).reshape(X, Y, Z)
        vyz[i, 0] = dot(tri[1], wz[0]).reshape(X, Y, Z)
        for x in range(X):
            stage_vy[i, 0, x:x + 1, :] = vyz[i, 0, x, 0:1, :]
            stage_vy[i, 1, x:x + 1, :] = vyz[i, 0, x, Y - 1:Y, :]
        made = [
            pair("gx", vx.at[i, X], vx.at[i, 0], vx.at[i, 1], vx.at[i, X + 1]),
            pair("gy", stage_vy.at[i, 1], rim_vy.at[i, 0], stage_vy.at[i, 0], rim_vy.at[i, 1]),
        ]
        for r in made:
            r.start()
        vyz[i, 1] = dot(tri[2], wz[1]).reshape(X, Y, Z)
        return made

    def keep(k, x, v):
        hi, lo = split(v)
        rows = pl.ds(pl.multiple_of(x * Y, Y), Y)
        tri[k, rows, 0:Z] = hi
        tri[k, rows, Z:2 * Z] = lo

    half = 0.5 * scale

    def faces_z(i):
        def step(x, carry):
            d, c, v = den[i, x], cot[i, x], vyz[i, 1, x]
            up = [pltpu.roll(t, Z - 1, 1) for t in (d, c, v)]
            lower, upper, bar = face_terms(d, up[0], c, up[1], v, up[2], valid_z)
            out[i, x] = c + (lower + pltpu.roll(upper, 1, 1))
            keep(2, x, half * (bar + pltpu.roll(bar, 1, 1)))
            return carry

        lax.fori_loop(0, X, step, 0)

    def faces_xy(i):
        first = face_terms(dcx[i, 0], dcx[i, 1], dcx[2 + i, 0], dcx[2 + i, 1], vx[i, 0], vx[i, 1], gx["has_lo"])

        def step(x, carry):
            upper_x, bar_x = carry
            d, c, v = dcx[i, x + 1], dcx[2 + i, x + 1], vx[i, x + 1]
            lower, upper, bar = face_terms(
                d, dcx[i, x + 2], c, dcx[2 + i, x + 2], v, vx[i, x + 2], (x < X - 1) | gx["has_hi"])
            total = lower + upper_x
            keep(0, x, half * (bar + bar_x))
            v = vyz[i, 0, x]
            one = pl.ds(x, 1)
            own = (d, c, v)
            below = (rim_y[0, i, one, :], rim_y[0, 2 + i, one, :], rim_vy[i, 0, one, :])
            above = (rim_y[1, i, one, :], rim_y[1, 2 + i, one, :], rim_vy[i, 1, one, :])
            up = [jnp.where(row == Y - 1, r, pltpu.roll(t, Y - 1, 0)) for t, r in zip(own, above)]
            ylower, yupper, ybar = face_terms(d, up[0], c, up[1], v, up[2], valid_y)
            _, eupper, ebar = face_terms(below[0], d[0:1], below[1], c[0:1], below[2], v[0:1], gy["has_lo"])
            total = total + ylower + jnp.where(row == 0, eupper, pltpu.roll(yupper, 1, 0))
            keep(1, x, half * (ybar + jnp.where(row == 0, ebar, pltpu.roll(ybar, 1, 0))))
            out[i, x] = out[i, x] + total
            return upper, bar

        lax.fori_loop(0, X, step, (first[1], first[2]))

    def backward(i):
        for k in range(3):
            zt[k] = dot(tri[k], wz[2 if k == 2 else 0]).reshape(X, Y, Z)

        def along_y(x, carry):
            va, vb, vc = (split(zt[k, x]) for k in range(3))
            blank = jnp.zeros((2 * Y, Z), BF16)
            rhs = jnp.concatenate([
                jnp.concatenate([vc[0], vc[1], vb[0], vb[1]], 0),
                jnp.concatenate([va[0], va[1], blank], 0)], 1)
            uv[x] = dot(wyt[...], rhs)
            return carry

        lax.fori_loop(0, X, along_y, 0, unroll=2)

        def along_x(k, carry):
            y0 = pl.multiple_of(k * 8, 8)
            q = [uv[c, pl.ds(y0, 8), 0:Z] for c in range(X)]
            p = [uv[c, pl.ds(y0, 8), Z:2 * Z] for c in range(X)]
            for j, v in enumerate(spread_rows(q, p)):
                spread[i, j, pl.ds(y0, 8), :] = v
            return carry

        lax.fori_loop(0, R // 8, along_x, 0)
        lax.fori_loop((R + Y) // 8, YE // 8, along_x, 0)
        made = []
        for part, only in ((slice(0, R), gy["has_lo"]), (slice(R + Y, YE), gy["has_hi"])):
            made.append(pair("gx", spread.at[i, R + X:XE, part], rx.at[i, 0, :, part],
                             spread.at[i, 0:R, part], rx.at[i, 1, :, part], only=only))
            made[-1].start()
        lax.fori_loop(R // 8, (R + Y) // 8, along_x, 0)
        centre = pair("gx", spread.at[i, R + X:XE, cy], rx.at[i, 0, :, cy],
                      spread.at[i, 0:R, cy], rx.at[i, 1, :, cy])
        centre.start()
        return made, centre

    def return_y(i, made):
        for m, part, has in ((made[0], slice(0, R), gy["has_lo"]), (made[1], slice(R + Y, YE), gy["has_hi"])):
            m.wait_recv()

            @pl.when(has)
            def _():
                spread[i, R:2 * R, part] = spread[i, R:2 * R, part] + rx[i, 0, :, part]
                spread[i, X:X + R, part] = spread[i, X:X + R, part] + rx[i, 1, :, part]
        back = pair("gy", spread.at[i, cx, R + Y:YE], ry.at[i, 0], spread.at[i, cx, 0:R], ry.at[i, 1])
        back.start()
        return back

    returned, centres, backs = [None, None], [None, None], [None, None]
    for i in range(2):
        to_x[i].wait_recv()
        for m in corners[i]:
            m.wait_recv()
        made = forward(i)
        faces_z(i)
        if i == 1:
            backs[0] = return_y(0, returned[0])
        if i == 0:
            for r in rims:
                r.wait_recv()
        for r in made:
            r.wait_recv()
        faces_xy(i)
        returned[i], centres[i] = backward(i)
    backs[1] = return_y(1, returned[1])
    for i in range(2):
        centres[i].wait_recv()
        spread[i, R:2 * R, cy] = spread[i, R:2 * R, cy] + rx[i, 0, :, cy]
        spread[i, X:X + R, cy] = spread[i, X:X + R, cy] + rx[i, 1, :, cy]
    for i in range(2):
        backs[i].wait_recv()
        spread[i, cx, R:2 * R] = spread[i, cx, R:2 * R] + ry[i, 0]
        spread[i, cx, Y:Y + R] = spread[i, cx, Y:Y + R] + ry[i, 1]

    def finish(x, carry):
        b = [spread[0, R + x, R:R + Y, :], spread[1, R + x, R:R + Y, :]]
        for i in range(2):
            out[i, x] = out[i, x] + (adh[0, i] * b[0] + adh[1, i] * b[1])
        return carry

    lax.fori_loop(0, X, finish, 0)
    for s in sends:
        s.wait_send()


def solution(mesh):
    nx, ny = mesh.shape["gx"], mesh.shape["gy"]

    def body(density, cotangent, adhesion):
        _, X, Y, Z = density.shape
        XE, YE = X + 2 * R, Y + 2 * R
        vmem = pl.BlockSpec(memory_space=pltpu.VMEM)
        return pl.pallas_call(
            lambda *refs: kernel(nx, ny, *refs),
            out_shape=jax.ShapeDtypeStruct(density.shape, F32),
            in_specs=[pl.BlockSpec(memory_space=pltpu.SMEM), vmem, vmem],
            out_specs=vmem,
            scratch_shapes=[
                pltpu.VMEM((2, XE, YE, Z), F32),
                pltpu.VMEM((X, YE, 2 * Z), F32),
                pltpu.VMEM((3, X * Y, 2 * Z), BF16),
                pltpu.VMEM((2, X + 2, Y, Z), F32),
                pltpu.VMEM((2, 2, X, Y, Z), F32),
                pltpu.VMEM((3, X, Y, Z), F32),
                pltpu.VMEM((4, X + 2, Y, Z), F32),
                pltpu.VMEM((2, 4, X, Z), F32),
                pltpu.VMEM((2, 4, X, Z), F32),
                pltpu.VMEM((2, 2, X, Z), F32),
                pltpu.VMEM((2, 2, X, Z), F32),
                pltpu.VMEM((2, XE, YE, Z), F32),
                pltpu.VMEM((2, 2, R, YE, Z), F32),
                pltpu.VMEM((2, 2, X, R, Z), F32),
                pltpu.VMEM((2 * Y, 2 * YE), BF16),
                pltpu.VMEM((YE, 4 * Y), BF16),
                pltpu.VMEM((3, 2 * Z, Z), BF16),
                pltpu.SemaphoreType.DMA((48,)),
                pltpu.SemaphoreType.DMA((48,)),
            ],
            compiler_params=pltpu.CompilerParams(
                collective_id=0, has_side_effects=True, vmem_limit_bytes=48 * 1024 * 1024
            ),
            cost_estimate=pl.CostEstimate(flops=10**9, bytes_accessed=3 * density.size * 4, transcendentals=0),
            name="adhesion_adjoint",
        )(adhesion, density, cotangent)

    spec = P(None, "gx", "gy", None)
    return jax.shard_map(body, mesh=mesh, in_specs=(spec, spec, P()), out_specs=spec, check_vma=False)
```

```python
import math

import jax
import jax.numpy as jnp
from jax import lax
from jax.experimental import pallas as pl
from jax.experimental.pallas import tpu as pltpu
from jax.sharding import PartitionSpec as P

R = 16
TIME_STEP = 0.5
SMOOTHING = 0.1
MESH = pl.DeviceIdType.MESH
F32 = jnp.float32
BF16 = jnp.bfloat16


def even_int(d):
    return jnp.maximum(R + 1.0 - jnp.abs(d), 0.0)


def odd_int(d):
    return even_int(d) * d


def weight_scale():
    e = sum((R + 1 - abs(d)) ** 2 for d in range(-R, R + 1))
    o = sum(((R + 1 - abs(d)) * d) ** 2 for d in range(-R, R + 1))
    return 1.0 / (math.sqrt(o) * e)


def offsets(rows, cols, lead):
    r = lax.broadcasted_iota(jnp.int32, (rows, cols), 0)
    c = lax.broadcasted_iota(jnp.int32, (rows, cols), 1)
    return (c - r - lead).astype(F32)


def split(v):
    hi = v.astype(BF16)
    return hi, (v - hi.astype(F32)).astype(BF16)


def dot(a, b):
    return lax.dot_general(a, b, (((1,), (0,)), ((), ())), preferred_element_type=F32)


def filter_rows(p, count):
    def box(k):
        s = p[k]
        for j in range(k + 1, k + R + 1):
            s = s + p[j]
        return s

    def start_odd(c):
        s = None
        for d in range(1, R + 1):
            t = float((R + 1 - d) * d) * (p[c + R + d] - p[c + R - d])
            s = t if s is None else s + t
        return s

    e0 = float(R + 1) * p[R]
    for d in range(1, R + 1):
        e0 = e0 + float(R + 1 - d) * (p[R + d] + p[R - d])
    even, odd = [e0], [start_odd(0), start_odd(1)]
    slope = odd[1] - odd[0]
    lo, hi = box(0), box(R + 1)
    for c in range(count - 1):
        if c > 0:
            lo = lo + (p[c + R] - p[c - 1])
            hi = hi + (p[c + 2 * R + 1] - p[c + R])
        delta = hi - lo
        even.append(even[-1] + delta)
        if c > 0:
            slope = slope + (
                (R + 2.0) * p[c + 2 * R + 1] - 2.0 * (delta + p[c + R]) - float(R) * p[c - 1]
            )
            odd.append(odd[-1] + slope)
    return even, odd


def spread_rows(q, p):
    n = len(q)

    def prefix(v):
        c = [None, v[0]]
        for k in range(1, n):
            c.append(c[-1] + v[k])
        return c

    cq, cp = prefix(q), prefix(p)

    def at(c, k):
        return c[min(max(k, 0), n)]

    def total(terms):
        s = None
        for w, v in terms:
            if v is None or w == 0.0:
                continue
            t = v if w == 1.0 else w * v
            s = t if s is None else s + t
        return s

    def plus(a, b):
        if a is None:
            return b
        return a if b is None else a + b

    out, slope, value = [], None, None
    for j in range(-1, n + 2 * R - 1):
        inner = [(1.0, at(cp, j + 1)), (-1.0, at(cp, j - R + 1)), (-1.0, at(cp, j - R)), (1.0, at(cp, j - 2 * R))]
        terms = {}
        for w, v in inner:
            if v is not None:
                terms[id(v)] = (terms.get(id(v), (0.0, v))[0] + 2.0 * w, v)
        terms = list(terms.values())
        if 0 <= j - 2 * R - 1 < n:
            terms.append((float(R), p[j - 2 * R - 1]))
        if 0 <= j + 1 < n:
            terms.append((-float(R), p[j + 1]))
        slope = plus(slope, total(terms))
        terms = {}
        for w, v in [(1.0, at(cq, j + 2)), (-2.0, at(cq, j - R + 1)), (1.0, at(cq, j - 2 * R))]:
            if v is not None:
                terms[id(v)] = (terms.get(id(v), (0.0, v))[0] + w, v)
        value = plus(value, plus(slope, total(list(terms.values()))))
        out.append(value)
    return out


def face_terms(lower_d, upper_d, lower_c, upper_c, lower_v, upper_v, valid):
    f = 0.5 * (lower_v + upper_v)
    square = f * f + SMOOTHING * SMOOTHING
    inverse = lax.rsqrt(square)
    magnitude = square * inverse
    bar = jnp.where(valid, (0.5 * TIME_STEP) * (upper_c - lower_c), 0.0)
    return (
        bar * (f + magnitude),
        bar * (f - magnitude),
        bar * ((lower_d + upper_d) - (f * inverse) * (upper_d - lower_d)),
    )


class Pair:
    def __init__(self, axis, place, src_up, dst_up, src_down, dst_down, send, recv, index, only=None):
        self.lo, self.hi = place["has_lo"], place["has_hi"]
        if only is not None:
            self.lo, self.hi = self.lo & only, self.hi & only
        self.up = pltpu.make_async_remote_copy(
            src_ref=src_up, dst_ref=dst_up, send_sem=send.at[index], recv_sem=recv.at[index],
            device_id={axis: place["hi"]}, device_id_type=MESH)
        self.down = pltpu.make_async_remote_copy(
            src_ref=src_down, dst_ref=dst_down, send_sem=send.at[index + 1], recv_sem=recv.at[index + 1],
            device_id={axis: place["lo"]}, device_id_type=MESH)

    def start(self):
        pl.when(self.hi)(lambda: self.up.start())
        pl.when(self.lo)(lambda: self.down.start())

    def wait_recv(self):
        pl.when(self.lo)(lambda: self.up.wait_recv())
        pl.when(self.hi)(lambda: self.down.wait_recv())

    def wait_send(self):
        pl.when(self.hi)(lambda: self.up.wait_send())
        pl.when(self.lo)(lambda: self.down.wait_send())


def place_on(axis, count):
    me = lax.axis_index(axis)
    return {
        "has_lo": me > 0,
        "has_hi": me < count - 1,
        "lo": jnp.maximum(me - 1, 0),
        "hi": jnp.minimum(me + 1, count - 1),
    }


def kernel(nx, ny, adh, den, cot, out, pot, uv, tri, vx, vyz, zt, dcx, rim_y, stage_y, rim_vy, stage_vy,
           spread, rx, ry, wy, wyt, wz, send, recv):
    X, Y, Z = den.shape[1:]
    XE, YE = X + 2 * R, Y + 2 * R
    gx, gy = place_on("gx", nx), place_on("gy", ny)
    scale = weight_scale()

    barrier = pltpu.get_barrier_semaphore()
    for axis, place in (("gx", gx), ("gy", gy)):
        for has, other in ((place["has_lo"], place["lo"]), (place["has_hi"], place["hi"])):
            @pl.when(has)
            def _():
                pl.semaphore_signal(barrier, inc=1, device_id={axis: other}, device_id_type=MESH)

    def zero(ref):
        ref[...] = jnp.zeros(ref.shape, ref.dtype)

    @pl.when(jnp.logical_not(gx["has_lo"]))
    def _():
        zero(pot.at[:, 0:R])
        zero(rx.at[:, 0])
        zero(dcx.at[:, 0:1])
        zero(vx.at[:, 0:1])

    @pl.when(jnp.logical_not(gx["has_hi"]))
    def _():
        zero(pot.at[:, R + X:])
        zero(rx.at[:, 1])
        zero(dcx.at[:, X + 1:])
        zero(vx.at[:, X + 1:])

    @pl.when(jnp.logical_not(gy["has_lo"]))
    def _():
        zero(pot.at[:, :, 0:R])
        zero(ry.at[:, 0])
        zero(rim_y.at[0])
        zero(rim_vy.at[:, 0])

    @pl.when(jnp.logical_not(gy["has_hi"]))
    def _():
        zero(pot.at[:, :, R + Y:])
        zero(ry.at[:, 1])
        zero(rim_y.at[1])
        zero(rim_vy.at[:, 1])

    a = [[adh[i, j] * scale for j in range(2)] for i in range(2)]

    def mix(x, carry):
        d = [den[0, x], den[1, x]]
        for i in range(2):
            pot[i, R + x, R:R + Y, :] = a[i][0] * d[0] + a[i][1] * d[1]
            dcx[i, 1 + x] = d[i]
            dcx[2 + i, 1 + x] = cot[i, x]
        return carry

    lax.fori_loop(0, X, mix, 0)
    for i in range(2):
        for x in range(X):
            stage_y[0, i, x:x + 1, :] = den[i, x, 0:1, :]
            stage_y[1, i, x:x + 1, :] = den[i, x, Y - 1:Y, :]
            stage_y[0, 2 + i, x:x + 1, :] = cot[i, x, 0:1, :]
            stage_y[1, 2 + i, x:x + 1, :] = cot[i, x, Y - 1:Y, :]

    peers = sum(place[has].astype(jnp.int32) for place in (gx, gy) for has in ("has_lo", "has_hi"))
    pl.semaphore_wait(barrier, peers)

    cx, cy = slice(R, R + X), slice(R, R + Y)
    sends = []
    counter = [0]

    def pair(axis, *refs, only=None):
        index = counter[0]
        counter[0] += 2
        made = Pair(axis, gx if axis == "gx" else gy, *refs, send, recv, index, only)
        sends.append(made)
        return made

    to_y, to_x = [], []
    for i in range(2):
        to_y.append(pair("gy", pot.at[i, cx, Y:Y + R], pot.at[i, cx, 0:R],
                         pot.at[i, cx, R:2 * R], pot.at[i, cx, R + Y:YE]))
        to_x.append(pair("gx", pot.at[i, X:X + R, cy], pot.at[i, 0:R, cy],
                         pot.at[i, R:2 * R, cy], pot.at[i, R + X:XE, cy]))
    rims = [
        pair("gx", dcx.at[:, X], dcx.at[:, 0], dcx.at[:, 1], dcx.at[:, X + 1]),
        pair("gy", stage_y.at[1], rim_y.at[0], stage_y.at[0], rim_y.at[1]),
    ]

    to_y[0].start()
    to_x[0].start()

    o = offsets(Y, YE, R)
    for k in range(2):
        wy[0:Y, k * YE:(k + 1) * YE] = even_int(o).astype(BF16)
        wy[Y:2 * Y, k * YE:(k + 1) * YE] = odd_int(o).astype(BF16)
    o = -offsets(YE, Y, -R)
    for k in range(2):
        wyt[:, k * Y:(k + 1) * Y] = even_int(o).astype(BF16)
        wyt[:, (2 + k) * Y:(3 + k) * Y] = odd_int(o).astype(BF16)
    o = offsets(Z, Z, 0)
    for k in range(2):
        wz[0, k * Z:(k + 1) * Z, :] = even_int(o).astype(BF16)
        wz[1, k * Z:(k + 1) * Z, :] = odd_int(-o).astype(BF16)
        wz[2, k * Z:(k + 1) * Z, :] = odd_int(o).astype(BF16)

    def send_corners(i):
        to_y[i].wait_recv()
        made = []
        for part, only in ((slice(0, R), gy["has_lo"]), (slice(R + Y, YE), gy["has_hi"])):
            made.append(pair("gx", pot.at[i, X:X + R, part], pot.at[i, 0:R, part],
                             pot.at[i, R:2 * R, part], pot.at[i, R + X:XE, part], only=only))
            made[-1].start()
        return made

    corners = [send_corners(0), None]
    to_y[1].start()
    for r in rims:
        r.start()

    row = lax.broadcasted_iota(jnp.int32, (Y, Z), 0)
    lane = lax.broadcasted_iota(jnp.int32, (Y, Z), 1)
    valid_z = lane < Z - 1
    valid_y = (row < Y - 1) | gy["has_hi"]

    def forward(i):
        def along_x(k, carry):
            y0 = pl.multiple_of(k * 8, 8)
            p = [pot[i, j, pl.ds(y0, 8), :] for j in range(XE)]
            even, odd = filter_rows(p, X)
            for c in range(X):
                uv[c, pl.ds(y0, 8), 0:Z] = even[c]
                uv[c, pl.ds(y0, 8), Z:2 * Z] = odd[c]
            return carry

        lax.fori_loop(0, YE // 8, along_x, 0)

        def along_y(x, carry):
            hi, lo = split(uv[x])
            r = dot(wy[...], jnp.concatenate([hi, lo], 0))
            rows = pl.ds(pl.multiple_of(x * Y, Y), Y)
            for k, v in enumerate((r[0:Y, Z:], r[Y:, 0:Z], r[0:Y, 0:Z])):
                hi, lo = split(v)
                tri[k, rows, 0:Z] = hi
                tri[k, rows, Z:2 * Z] = lo
            return carry

        lax.fori_loop(0, X, along_y, 0, unroll=2)
        vx[i, 1:X + 1] = dot(tri[0], wz[0]).reshape(X, Y, Z)
        vyz[i, 0] = dot(tri[1], wz[0]).reshape(X, Y, Z)
        for x in range(X):
            stage_vy[i, 0, x:x + 1, :] = vyz[i, 0, x, 0:1, :]
            stage_vy[i, 1, x:x + 1, :] = vyz[i, 0, x, Y - 1:Y, :]
        made = [
            pair("gx", vx.at[i, X], vx.at[i, 0], vx.at[i, 1], vx.at[i, X + 1]),
            pair("gy", stage_vy.at[i, 1], rim_vy.at[i, 0], stage_vy.at[i, 0], rim_vy.at[i, 1]),
        ]
        for r in made:
            r.start()
        vyz[i, 1] = dot(tri[2], wz[1]).reshape(X, Y, Z)
        return made

    def keep(k, x, v):
        hi, lo = split(v)
        rows = pl.ds(pl.multiple_of(x * Y, Y), Y)
        tri[k, rows, 0:Z] = hi
        tri[k, rows, Z:2 * Z] = lo

    half = 0.5 * scale

    def faces_z(i):
        def step(x, carry):
            d, c, v = den[i, x], cot[i, x], vyz[i, 1, x]
            up = [pltpu.roll(t, Z - 1, 1) for t in (d, c, v)]
            lower, upper, bar = face_terms(d, up[0], c, up[1], v, up[2], valid_z)
            out[i, x] = c + (lower + pltpu.roll(upper, 1, 1))
            keep(2, x, half * (bar + pltpu.roll(bar, 1, 1)))
            return carry

        lax.fori_loop(0, X, step, 0)

    def faces_xy(i):
        first = face_terms(dcx[i, 0], dcx[i, 1], dcx[2 + i, 0], dcx[2 + i, 1], vx[i, 0], vx[i, 1], gx["has_lo"])

        def step(x, carry):
            upper_x, bar_x = carry
            d, c, v = dcx[i, x + 1], dcx[2 + i, x + 1], vx[i, x + 1]
            lower, upper, bar = face_terms(
                d, dcx[i, x + 2], c, dcx[2 + i, x + 2], v, vx[i, x + 2], (x < X - 1) | gx["has_hi"])
            total = lower + upper_x
            keep(0, x, half * (bar + bar_x))
            v = vyz[i, 0, x]
            one = pl.ds(x, 1)
            own = (d, c, v)
            below = (rim_y[0, i, one, :], rim_y[0, 2 + i, one, :], rim_vy[i, 0, one, :])
            above = (rim_y[1, i, one, :], rim_y[1, 2 + i, one, :], rim_vy[i, 1, one, :])
            up = [jnp.where(row == Y - 1, r, pltpu.roll(t, Y - 1, 0)) for t, r in zip(own, above)]
            ylower, yupper, ybar = face_terms(d, up[0], c, up[1], v, up[2], valid_y)
            _, eupper, ebar = face_terms(below[0], d[0:1], below[1], c[0:1], below[2], v[0:1], gy["has_lo"])
            total = total + ylower + jnp.where(row == 0, eupper, pltpu.roll(yupper, 1, 0))
            keep(1, x, half * (ybar + jnp.where(row == 0, ebar, pltpu.roll(ybar, 1, 0))))
            out[i, x] = out[i, x] + total
            return upper, bar

        lax.fori_loop(0, X, step, (first[1], first[2]))

    def backward(i):
        for k in range(3):
            zt[k] = dot(tri[k], wz[2 if k == 2 else 0]).reshape(X, Y, Z)

        def along_y(x, carry):
            va, vb, vc = (split(zt[k, x]) for k in range(3))
            blank = jnp.zeros((2 * Y, Z), BF16)
            rhs = jnp.concatenate([
                jnp.concatenate([vc[0], vc[1], vb[0], vb[1]], 0),
                jnp.concatenate([va[0], va[1], blank], 0)], 1)
            uv[x] = dot(wyt[...], rhs)
            return carry

        lax.fori_loop(0, X, along_y, 0, unroll=2)

        def along_x(k, carry):
            y0 = pl.multiple_of(k * 8, 8)
            q = [uv[c, pl.ds(y0, 8), 0:Z] for c in range(X)]
            p = [uv[c, pl.ds(y0, 8), Z:2 * Z] for c in range(X)]
            for j, v in enumerate(spread_rows(q, p)):
                spread[i, j, pl.ds(y0, 8), :] = v
            return carry

        lax.fori_loop(0, R // 8, along_x, 0)
        lax.fori_loop((R + Y) // 8, YE // 8, along_x, 0)
        made = []
        for part, only in ((slice(0, R), gy["has_lo"]), (slice(R + Y, YE), gy["has_hi"])):
            made.append(pair("gx", spread.at[i, R + X:XE, part], rx.at[i, 0, :, part],
                             spread.at[i, 0:R, part], rx.at[i, 1, :, part], only=only))
            made[-1].start()
        lax.fori_loop(R // 8, (R + Y) // 8, along_x, 0)
        centre = pair("gx", spread.at[i, R + X:XE, cy], rx.at[i, 0, :, cy],
                      spread.at[i, 0:R, cy], rx.at[i, 1, :, cy])
        return made, centre

    def return_y(i, made):
        for m, part, has in ((made[0], slice(0, R), gy["has_lo"]), (made[1], slice(R + Y, YE), gy["has_hi"])):
            m.wait_recv()

            @pl.when(has)
            def _():
                spread[i, R:2 * R, part] = spread[i, R:2 * R, part] + rx[i, 0, :, part]
                spread[i, X:X + R, part] = spread[i, X:X + R, part] + rx[i, 1, :, part]
        back = pair("gy", spread.at[i, cx, R + Y:YE], ry.at[i, 0], spread.at[i, cx, 0:R], ry.at[i, 1])
        back.start()
        return back

    returned, centres, backs = [None, None], [None, None], [None, None]
    for i in range(2):
        to_x[i].wait_recv()
        for m in corners[i]:
            m.wait_recv()
        if i == 0:
            to_x[1].start()
        made = forward(i)
        faces_z(i)
        if i == 1:
            backs[0] = return_y(0, returned[0])
            centres[0].start()
        if i == 0:
            corners[1] = send_corners(1)
            for r in rims:
                r.wait_recv()
        for r in made:
            r.wait_recv()
        faces_xy(i)
        returned[i], centres[i] = backward(i)
    backs[1] = return_y(1, returned[1])
    centres[1].start()
    for i in range(2):
        centres[i].wait_recv()
        spread[i, R:2 * R, cy] = spread[i, R:2 * R, cy] + rx[i, 0, :, cy]
        spread[i, X:X + R, cy] = spread[i, X:X + R, cy] + rx[i, 1, :, cy]
    for i in range(2):
        backs[i].wait_recv()
        spread[i, cx, R:2 * R] = spread[i, cx, R:2 * R] + ry[i, 0]
        spread[i, cx, Y:Y + R] = spread[i, cx, Y:Y + R] + ry[i, 1]

    def finish(x, carry):
        b = [spread[0, R + x, R:R + Y, :], spread[1, R + x, R:R + Y, :]]
        for i in range(2):
            out[i, x] = out[i, x] + (adh[0, i] * b[0] + adh[1, i] * b[1])
        return carry

    lax.fori_loop(0, X, finish, 0)
    for s in sends:
        s.wait_send()


def solution(mesh):
    nx, ny = mesh.shape["gx"], mesh.shape["gy"]

    def body(density, cotangent, adhesion):
        _, X, Y, Z = density.shape
        XE, YE = X + 2 * R, Y + 2 * R
        vmem = pl.BlockSpec(memory_space=pltpu.VMEM)
        return pl.pallas_call(
            lambda *refs: kernel(nx, ny, *refs),
            out_shape=jax.ShapeDtypeStruct(density.shape, F32),
            in_specs=[pl.BlockSpec(memory_space=pltpu.SMEM), vmem, vmem],
            out_specs=vmem,
            scratch_shapes=[
                pltpu.VMEM((2, XE, YE, Z), F32),
                pltpu.VMEM((X, YE, 2 * Z), F32),
                pltpu.VMEM((3, X * Y, 2 * Z), BF16),
                pltpu.VMEM((2, X + 2, Y, Z), F32),
                pltpu.VMEM((2, 2, X, Y, Z), F32),
                pltpu.VMEM((3, X, Y, Z), F32),
                pltpu.VMEM((4, X + 2, Y, Z), F32),
                pltpu.VMEM((2, 4, X, Z), F32),
                pltpu.VMEM((2, 4, X, Z), F32),
                pltpu.VMEM((2, 2, X, Z), F32),
                pltpu.VMEM((2, 2, X, Z), F32),
                pltpu.VMEM((2, XE, YE, Z), F32),
                pltpu.VMEM((2, 2, R, YE, Z), F32),
                pltpu.VMEM((2, 2, X, R, Z), F32),
                pltpu.VMEM((2 * Y, 2 * YE), BF16),
                pltpu.VMEM((YE, 4 * Y), BF16),
                pltpu.VMEM((3, 2 * Z, Z), BF16),
                pltpu.SemaphoreType.DMA((48,)),
                pltpu.SemaphoreType.DMA((48,)),
            ],
            compiler_params=pltpu.CompilerParams(
                collective_id=0, has_side_effects=True, vmem_limit_bytes=48 * 1024 * 1024
            ),
            cost_estimate=pl.CostEstimate(flops=10**9, bytes_accessed=3 * density.size * 4, transcendentals=0),
            name="adhesion_adjoint",
        )(adhesion, density, cotangent)

    spec = P(None, "gx", "gy", None)
    return jax.shard_map(body, mesh=mesh, in_specs=(spec, spec, P()), out_specs=spec, check_vma=False)
```
